32 devices in a mesh: seq: 8 (over z, core), ch: 4 (over y, x).
Axes of the slice: x: 2, y: 2, z: 4, core: 2. Of those that a mesh axis runs over, the one named last changes fastest.
Arguments:
- tokens: bfloat16 [8192, 4096], P('seq', 'ch'), may hold values from -6 to 6
- w_in: bfloat16 [4096, 3, 4096], P(None, None, 'ch'), may hold values from -0.09375 to 0.09375
- w_short: float32 [3, 3, 4096], P(None, None, 'ch'), may hold values from -3.5 to 3.5
- skip_gain: float32 [4096], P('ch'), may hold values from 0.5 to 1.5
- filter_spectra: bfloat16 [2, 16, 1024, 4096], P(None, 'seq', None, 'ch'), may hold values from -6 to 6
- w_out: bfloat16 [4096, 4096], P('ch'), may hold values from -0.09375 to 0.09375
Outputs:
- mixed_out: bfloat16 [8192, 4096], P(('seq', 'ch'))
The draws below stay inside these ranges and needn't reach their ends.
All inputs are finite; a program needn't handle non-finite values.
Results may differ from the reference program's by a relative error of at most 0.015.
Values may be sent and summed in bfloat16 or wider, within the bound.
A program may use at most 256 MiB of HBM per device.

```python
import jax
import jax.numpy as jnp
from jax import lax

D = 4096
TOK_DEV = 1024
LENGTH = 8192
BINS = 16
N_CH = 4


def block_levels(stream_key, extent, split, least, largest):
    def one(dim, shards_of):
        draws = jax.random.uniform(jax.random.fold_in(jax.random.fold_in(stream_key, 6), dim), (shards_of,), jnp.float32, least / len(split), largest / len(split))
        return jnp.repeat(jnp.exp(draws), extent[dim] // shards_of).reshape((-1,) + (1,) * (len(extent) - dim - 1))

    gain = one(*split[0])
    for cut in split[1:]:
        gain = gain * one(*cut)
    return gain


def gaussian(own_key, shape, spread, limit, split=(), held_as=jnp.bfloat16):
    entries = jax.random.normal(own_key, shape, jnp.float32) * spread
    if len(split) > 0:
        entries = block_levels(own_key, shape, split, -0.22, 0.18) * entries
    return jnp.clip(entries, min=-limit, max=limit).astype(held_as)


def setup_inputs(seed: int = 0) -> dict:
    arg_keys = jax.random.split(jax.random.key(seed), 7)
    return {
        "tokens": gaussian(arg_keys[0], (LENGTH, D), 1.0, 6.0, ((0, 8), (1, 4))),
        "w_in": gaussian(arg_keys[1], (D, 3, D), D ** -0.5, 0.09375, ((2, 4),)),
        "w_short": gaussian(arg_keys[2], (3, 3, D), 3 ** -0.5, 3.5, ((2, 4),), jnp.float32),
        "skip_gain": jnp.clip(0.5 + 1.0 * jax.random.uniform(arg_keys[3], (D,), jnp.float32) ** block_levels(arg_keys[3], (D,), ((0, 4),), -0.2, 0.2), 0.5, 1.5),
        "filter_spectra": gaussian(arg_keys[4], (2, BINS, TOK_DEV, D), 1.0, 6.0, ((1, 8), (3, 4))),
        "w_out": gaussian(arg_keys[5], (D, D), D ** -0.5, 0.09375, ((0, 4),)),
    }


def reference(tokens, w_in, w_short, skip_gain, filter_spectra, w_out):
    projected = jnp.dot(tokens, w_in.reshape(D, 3 * D), preferred_element_type=jnp.float32).astype(jnp.bfloat16)
    projected = lax.optimization_barrier(projected)
    projected = projected.reshape(LENGTH, 3, D).astype(jnp.float32)
    extended = jnp.concatenate([jnp.zeros((2, 3, D), jnp.float32), projected], 0)
    tap_weights = w_short.astype(jnp.float32)
    streams = tap_weights[0] * extended[2:] + tap_weights[1] * extended[1:-1] + tap_weights[2] * extended[:-2]
    signal = (streams[:, 0] * streams[:, 2]).astype(jnp.bfloat16)
    group_size = D // N_CH
    total_sum = jnp.zeros((LENGTH, D), jnp.float32)
    for group_id in range(N_CH):
        first_col = group_id * group_size
        last_col = first_col + group_size
        group_signal = signal[:, first_col:last_col].astype(jnp.float32)
        padded = jnp.concatenate([group_signal, jnp.zeros_like(group_signal)], 0)
        response_table = filter_spectra[:, :, :, first_col:last_col].astype(jnp.float32)
        response_table = response_table.transpose(0, 2, 1, 3).reshape(2, 2 * LENGTH, group_size)
        spectrum = jnp.fft.fft(padded, axis=0) * (response_table[0] + 1j * response_table[1])
        convolved = jnp.real(jnp.fft.ifft(spectrum, axis=0))[:LENGTH]
        response = convolved + skip_gain[first_col:last_col].astype(jnp.float32) * group_signal
        gated_out = (streams[:, 1, first_col:last_col] * response).astype(jnp.bfloat16)
        partial_term = jnp.dot(gated_out, w_out[first_col:last_col], preferred_element_type=jnp.float32)
        rounded_term = lax.optimization_barrier(partial_term.astype(jnp.bfloat16))
        total_sum = total_sum + rounded_term.astype(jnp.float32)
    return total_sum.astype(jnp.bfloat16)
```

```python
import math

import jax
import jax.numpy as jnp
import ml_dtypes
import numpy as np
from jax import lax
from jax.sharding import PartitionSpec as P

TWO_PI = 2.0 * math.pi
BF16 = jnp.bfloat16
F32 = jnp.float32


def shifted(array, axis, by):
    count = lax.axis_size(axis)
    pairs = [(i, i + by) for i in range(count) if 0 <= i + by < count]
    return lax.ppermute(array, axis, pairs)


def dense_transform(size):
    product = np.outer(np.arange(size), np.arange(size)) % size
    angle = product * (TWO_PI / size)
    cos, sin = np.cos(angle), np.sin(angle)
    return np.block([[cos, sin], [-sin, cos]]).astype(ml_dtypes.bfloat16)


def phases(left, right, modulus):
    product = left[:, None] * right[None, :] % modulus
    angle = product.astype(F32) * (TWO_PI / modulus)
    return jnp.cos(angle), jnp.sin(angle)


def spread_filter(filter_spectra, seq_pos, seq_count):
    _, own, row_count, channels = filter_spectra.shape
    share = channels // seq_count
    pieces = []
    for k in range(seq_count):
        first = (seq_pos + k) % seq_count * share
        piece = lax.dynamic_slice_in_dim(filter_spectra, first, share, 3)
        if k:
            pairs = [(s, (s + k) % seq_count) for s in range(seq_count)]
            piece = lax.ppermute(piece, "seq", pairs)
        pieces.append(piece)
    return pieces


def on_device(tokens, w_in, w_short, skip_gain, filter_spectra, w_out):
    row_count = tokens.shape[0]
    channels = w_in.shape[2]
    seq_count = lax.axis_size("seq")
    seq_pos = lax.axis_index("seq")
    bin_count = 2 * seq_count
    share = channels // seq_count
    fft_length = bin_count * row_count

    pieces = spread_filter(filter_spectra, seq_pos, seq_count)

    gathered = lax.all_gather(tokens, "ch", axis=1, tiled=True)
    projected = [
        jnp.dot(gathered, w_in[:, s], preferred_element_type=F32).astype(BF16) for s in range(3)
    ]
    before = shifted(jnp.stack([p[row_count - 2 :] for p in projected]), "seq", 1)

    def stream(s):
        extended = jnp.concatenate([before[s], projected[s]], 0).astype(F32)
        taps = w_short[:, s]
        return taps[0] * extended[2:] + taps[1] * extended[1:-1] + taps[2] * extended[:-2]

    signal = (stream(0) * stream(2)).astype(BF16)
    second_gate = stream(1)

    columns = lax.all_to_all(
        signal.reshape(row_count, seq_count, share).transpose(1, 0, 2),
        "seq",
        split_axis=0,
        concat_axis=0,
        tiled=True,
    )
    senders = (seq_pos - jnp.arange(seq_count, dtype=jnp.int32)) % seq_count
    classes = (senders[:, None] * 2 + jnp.arange(2, dtype=jnp.int32)[None, :]).reshape(-1)
    cos_block, sin_block = phases(classes, jnp.arange(seq_count, dtype=jnp.int32), bin_count)
    cos_twist, sin_twist = phases(jnp.arange(row_count, dtype=jnp.int32), classes, fft_length)
    cos_twist, sin_twist = cos_twist[:, :, None], sin_twist[:, :, None]
    table = jnp.asarray(dense_transform(row_count))

    real = jnp.einsum("kp,pbc->bkc", cos_block.astype(BF16), columns, preferred_element_type=F32)
    imag = -jnp.einsum("kp,pbc->bkc", sin_block.astype(BF16), columns, preferred_element_type=F32)
    real, imag = (
        real * cos_twist + imag * sin_twist,
        imag * cos_twist - real * sin_twist,
    )
    packed = jnp.concatenate([real.astype(BF16), imag.astype(BF16)], 0)
    packed = packed.reshape(2 * row_count, bin_count * share)
    spectrum = jnp.dot(table, packed, preferred_element_type=F32).astype(BF16)
    spectrum = spectrum.reshape(2, row_count, bin_count, share).astype(F32)

    response = jnp.concatenate(pieces, 1).transpose(0, 2, 1, 3).astype(F32)
    real = spectrum[0] * response[0] - spectrum[1] * response[1]
    imag = spectrum[0] * response[1] + spectrum[1] * response[0]
    packed = jnp.concatenate([real.astype(BF16), imag.astype(BF16)], 0)
    packed = packed.reshape(2 * row_count, bin_count * share)
    partial = lax.dot_general(
        table, packed, (((0,), (0,)), ((), ())), preferred_element_type=F32
    ).astype(BF16)
    partial = partial.reshape(2, row_count, bin_count, share).astype(F32)
    scale = 1.0 / fft_length
    real = ((partial[0] * cos_twist - partial[1] * sin_twist) * scale).astype(BF16)
    imag = ((partial[1] * cos_twist + partial[0] * sin_twist) * scale).astype(BF16)
    convolved = jnp.einsum(
        "kp,bkc->pbc", cos_block.astype(BF16), real, preferred_element_type=F32
    ) - jnp.einsum("kp,bkc->pbc", sin_block.astype(BF16), imag, preferred_element_type=F32)
    convolved = lax.all_to_all(
        convolved.astype(BF16), "seq", split_axis=0, concat_axis=0, tiled=True
    )
    convolved = convolved.transpose(1, 0, 2).reshape(row_count, channels).astype(F32)

    response = convolved + skip_gain * signal.astype(F32)
    gated_out = (second_gate * response).astype(BF16)
    return lax.psum_scatter(
        jnp.dot(gated_out, w_out, preferred_element_type=F32).astype(BF16),
        "ch",
        scatter_dimension=0,
        tiled=True,
    )


def solution(mesh):
    return jax.shard_map(
        on_device,
        mesh=mesh,
        in_specs=(
            P("seq", "ch"),
            P(None, None, "ch"),
            P(None, None, "ch"),
            P("ch"),
            P(None, "seq", None, "ch"),
            P("ch", None),
        ),
        out_specs=P(("seq", "ch"), None),
        check_vma=False,
    )
```

```python
import math

import jax
import jax.numpy as jnp
import ml_dtypes
import numpy as np
from jax import lax
from jax.experimental import pallas as pl
from jax.experimental.pallas import tpu as pltpu
from jax.sharding import PartitionSpec as P

TWO_PI = 2.0 * math.pi
BF16 = jnp.bfloat16
F32 = jnp.float32


def shifted(array, axis, by):
    count = lax.axis_size(axis)
    pairs = [(i, i + by) for i in range(count) if 0 <= i + by < count]
    return lax.ppermute(array, axis, pairs)


def dense_transform(size):
    product = np.outer(np.arange(size), np.arange(size)) % size
    angle = product * (TWO_PI / size)
    cos, sin = np.cos(angle), np.sin(angle)
    return np.block([[cos, sin], [-sin, cos]]).astype(ml_dtypes.bfloat16)


def phases(left, right, modulus):
    product = left[:, None] * right[None, :] % modulus
    angle = product.astype(F32) * (TWO_PI / modulus)
    return jnp.cos(angle), jnp.sin(angle)


def spread_filter(filter_spectra, seq_pos, seq_count):
    _, own, row_count, channels = filter_spectra.shape
    share = channels // seq_count
    pieces = []
    for k in range(seq_count):
        first = (seq_pos + k) % seq_count * share
        piece = lax.dynamic_slice_in_dim(filter_spectra, first, share, 3)
        if k:
            pairs = [(s, (s + k) % seq_count) for s in range(seq_count)]
            piece = lax.ppermute(piece, "seq", pairs)
        pieces.append(piece)
    return pieces


def long_filter(cos_ref, sin_ref, x_ref, ct_ref, st_ref, h_ref, table_ref, out_ref, acc, left, right):
    blocks, row_count, share = x_ref.shape
    step = pl.program_id(0)
    chunk, tile = 64, 512

    @pl.when(step == 0)
    def _():
        acc[...] = jnp.zeros_like(acc)

    @pl.loop(0, row_count // chunk)
    def _(c):
        rows = pl.ds(pl.multiple_of(c * chunk, chunk), chunk)
        below = pl.ds(pl.multiple_of(row_count + c * chunk, chunk), chunk)
        x = [x_ref[p, rows, :].astype(F32) for p in range(blocks)]
        for q in range(2):
            real = x[0]
            imag = jnp.zeros_like(real)
            for p in range(1, blocks):
                real = real + cos_ref[2 * step + q, p] * x[p]
                imag = imag - sin_ref[2 * step + q, p] * x[p]
            ct, st = ct_ref[q, rows, :], st_ref[q, rows, :]
            lanes = slice(q * share, (q + 1) * share)
            left[rows, lanes] = (real * ct + imag * st).astype(BF16)
            left[below, lanes] = (imag * ct - real * st).astype(BF16)

    @pl.loop(0, row_count // tile)
    def _(m):
        rows = pl.ds(pl.multiple_of(m * tile, tile), tile)
        below = pl.ds(pl.multiple_of(row_count + m * tile, tile), tile)
        real = jnp.dot(table_ref[rows, :], left[...], preferred_element_type=F32)
        imag = jnp.dot(table_ref[below, :], left[...], preferred_element_type=F32)
        for q in range(2):
            lanes = slice(q * share, (q + 1) * share)
            a, b = real[:, lanes], imag[:, lanes]
            hr, hi = h_ref[0, 0, q, rows, :].astype(F32), h_ref[0, 1, q, rows, :].astype(F32)
            right[rows, lanes] = (a * hr - b * hi).astype(BF16)
            right[below, lanes] = (-(a * hi + b * hr)).astype(BF16)

    @pl.loop(0, row_count // tile)
    def _(m):
        rows = pl.ds(pl.multiple_of(m * tile, tile), tile)
        below = pl.ds(pl.multiple_of(row_count + m * tile, tile), tile)
        real = jnp.dot(table_ref[rows, :], right[...], preferred_element_type=F32)
        imag = jnp.dot(table_ref[below, :], right[...], preferred_element_type=F32)
        turned = []
        for q in range(2):
            lanes = slice(q * share, (q + 1) * share)
            a, b = real[:, lanes], imag[:, lanes]
            ct, st = ct_ref[q, rows, :], st_ref[q, rows, :]
            turned.append((a * ct + b * st, a * st - b * ct))
        for p in range(blocks):
            total = acc[p, rows, :]
            for q in range(2):
                total = total + cos_ref[2 * step + q, p] * turned[q][0]
                total = total - sin_ref[2 * step + q, p] * turned[q][1]
            acc[p, rows, :] = total

    @pl.when(step == pl.num_programs(0) - 1)
    def _():
        scale = 1.0 / (2 * blocks * row_count)
        out_ref[...] = (acc[...] * scale).astype(BF16)


def call_long_filter(cos_block, sin_block, columns, cos_twist, sin_twist, response, table):
    blocks, row_count, share = columns.shape
    whole = lambda *shape: pl.BlockSpec(shape, lambda k: (0,) * len(shape))
    twist = pl.BlockSpec((2, row_count, share), lambda k: (k, 0, 0))
    flops = 2 * blocks * 2 * (2 * row_count) ** 2 * (2 * share)
    return pl.pallas_call(
        long_filter,
        grid=(blocks,),
        out_shape=jax.ShapeDtypeStruct(columns.shape, BF16),
        in_specs=[
            pl.BlockSpec(memory_space=pltpu.SMEM),
            pl.BlockSpec(memory_space=pltpu.SMEM),
            whole(blocks, row_count, share),
            twist,
            twist,
            pl.BlockSpec((1, 2, 2, row_count, share), lambda k: (k, 0, 0, 0, 0)),
            whole(2 * row_count, 2 * row_count),
        ],
        out_specs=whole(blocks, row_count, share),
        scratch_shapes=[
            pltpu.VMEM((blocks, row_count, share), F32),
            pltpu.VMEM((2 * row_count, 2 * share), BF16),
            pltpu.VMEM((2 * row_count, 2 * share), BF16),
        ],
        compiler_params=pltpu.CompilerParams(vmem_limit_bytes=56 * 2**20),
        cost_estimate=pl.CostEstimate(flops=flops, bytes_accessed=40 * 2**20, transcendentals=0),
    )(cos_block, sin_block, columns, cos_twist, sin_twist, response, table)


def on_device(tokens, w_in, w_short, skip_gain, filter_spectra, w_out):
    row_count = tokens.shape[0]
    channels = w_in.shape[2]
    seq_count = lax.axis_size("seq")
    seq_pos = lax.axis_index("seq")
    bin_count = 2 * seq_count
    share = channels // seq_count
    fft_length = bin_count * row_count

    pieces = spread_filter(filter_spectra, seq_pos, seq_count)

    gathered = lax.all_gather(tokens, "ch", axis=1, tiled=True)
    early = 1 + (seq_count - 1) * 4 // 7
    gathered, pieces[1:early] = lax.optimization_barrier((gathered, pieces[1:early]))
    projected = [
        jnp.dot(gathered, w_in[:, s], preferred_element_type=F32).astype(BF16) for s in range(3)
    ]
    before = shifted(jnp.stack([p[row_count - 2 :] for p in projected]), "seq", 1)

    def stream(s):
        extended = jnp.concatenate([before[s], projected[s]], 0).astype(F32)
        taps = w_short[:, s]
        return taps[0] * extended[2:] + taps[1] * extended[1:-1] + taps[2] * extended[:-2]

    signal = (stream(0) * stream(2)).astype(BF16)
    signal, pieces[early:] = lax.optimization_barrier((signal, pieces[early:]))
    second_gate = stream(1)

    columns = lax.all_to_all(
        signal.reshape(row_count, seq_count, share).transpose(1, 0, 2),
        "seq",
        split_axis=0,
        concat_axis=0,
        tiled=True,
    )
    senders = (seq_pos - jnp.arange(seq_count, dtype=jnp.int32)) % seq_count
    classes = (senders[:, None] * 2 + jnp.arange(2, dtype=jnp.int32)[None, :]).reshape(-1)
    cos_block, sin_block = phases(classes, jnp.arange(seq_count, dtype=jnp.int32), bin_count)
    cos_twist, sin_twist = phases(classes, jnp.arange(row_count, dtype=jnp.int32), fft_length)
    twist_shape = (bin_count, row_count, share)
    convolved = call_long_filter(
        cos_block,
        sin_block,
        columns,
        jnp.broadcast_to(cos_twist[:, :, None], twist_shape),
        jnp.broadcast_to(sin_twist[:, :, None], twist_shape),
        jnp.stack(pieces),
        jnp.asarray(dense_transform(row_count)),
    )
    convolved = lax.all_to_all(
        convolved, "seq", split_axis=0, concat_axis=0, tiled=True
    )
    convolved = convolved.transpose(1, 0, 2).reshape(row_count, channels).astype(F32)

    response = convolved + skip_gain * signal.astype(F32)
    gated_out = (second_gate * response).astype(BF16)
    return lax.psum_scatter(
        jnp.dot(gated_out, w_out, preferred_element_type=F32).astype(BF16),
        "ch",
        scatter_dimension=0,
        tiled=True,
    )


def solution(mesh):
    return jax.shard_map(
        on_device,
        mesh=mesh,
        in_specs=(
            P("seq", "ch"),
            P(None, None, "ch"),
            P(None, None, "ch"),
            P("ch"),
            P(None, "seq", None, "ch"),
            P("ch", None),
        ),
        out_specs=P(("seq", "ch"), None),
        check_vma=False,
    )
```

```python
import math

import jax
import jax.numpy as jnp
import ml_dtypes
import numpy as np
from jax import lax
from jax.experimental import pallas as pl
from jax.experimental.pallas import tpu as pltpu
from jax.sharding import PartitionSpec as P

TWO_PI = 2.0 * math.pi
BF16 = jnp.bfloat16
F32 = jnp.float32


def shifted(array, axis, by):
    count = lax.axis_size(axis)
    pairs = [(i, i + by) for i in range(count) if 0 <= i + by < count]
    return lax.ppermute(array, axis, pairs)


def dense_transform(size):
    product = np.outer(np.arange(size), np.arange(size)) % size
    angle = product * (TWO_PI / size)
    cos, sin = np.cos(angle), np.sin(angle)
    return np.block([[cos, sin], [-sin, cos]]).astype(ml_dtypes.bfloat16)


def phases(left, right, modulus):
    product = left[:, None] * right[None, :] % modulus
    angle = product.astype(F32) * (TWO_PI / modulus)
    return jnp.cos(angle), jnp.sin(angle)


def spread_filter(filter_spectra, own):
    _, _, row_count, channels = filter_spectra.shape
    seq_count = lax.axis_size("seq")
    pieces = filter_spectra[:, own].reshape(2, row_count, seq_count, channels // seq_count)
    return lax.all_to_all(
        pieces.transpose(2, 0, 1, 3), "seq", split_axis=0, concat_axis=0, tiled=True
    )


def long_filter(cos_ref, sin_ref, x_ref, ct_ref, st_ref, h0_ref, h1_ref, table_ref, out_ref, acc, left, right):
    blocks, row_count, share = x_ref.shape
    step = pl.program_id(0)
    chunk, tile = 64, 512

    @pl.when(step == 0)
    def _():
        acc[...] = jnp.zeros_like(acc)

    @pl.loop(0, row_count // chunk)
    def _(c):
        rows = pl.ds(pl.multiple_of(c * chunk, chunk), chunk)
        below = pl.ds(pl.multiple_of(row_count + c * chunk, chunk), chunk)
        x = [x_ref[p, rows, :].astype(F32) for p in range(blocks)]
        for q in range(2):
            real = x[0]
            imag = jnp.zeros_like(real)
            for p in range(1, blocks):
                real = real + cos_ref[2 * step + q, p] * x[p]
                imag = imag - sin_ref[2 * step + q, p] * x[p]
            ct, st = ct_ref[q, rows, :], st_ref[q, rows, :]
            lanes = slice(q * share, (q + 1) * share)
            left[rows, lanes] = (real * ct + imag * st).astype(BF16)
            left[below, lanes] = (imag * ct - real * st).astype(BF16)

    @pl.loop(0, row_count // tile)
    def _(m):
        rows = pl.ds(pl.multiple_of(m * tile, tile), tile)
        below = pl.ds(pl.multiple_of(row_count + m * tile, tile), tile)
        real = jnp.dot(table_ref[rows, :], left[...], preferred_element_type=F32)
        imag = jnp.dot(table_ref[below, :], left[...], preferred_element_type=F32)
        for q in range(2):
            lanes = slice(q * share, (q + 1) * share)
            a, b = real[:, lanes], imag[:, lanes]
            h_ref = (h0_ref, h1_ref)[q]
            hr, hi = h_ref[0, 0, rows, :].astype(F32), h_ref[0, 1, rows, :].astype(F32)
            right[rows, lanes] = (a * hr - b * hi).astype(BF16)
            right[below, lanes] = (-(a * hi + b * hr)).astype(BF16)

    @pl.loop(0, row_count // tile)
    def _(m):
        rows = pl.ds(pl.multiple_of(m * tile, tile), tile)
        below = pl.ds(pl.multiple_of(row_count + m * tile, tile), tile)
        real = jnp.dot(table_ref[rows, :], right[...], preferred_element_type=F32)
        imag = jnp.dot(table_ref[below, :], right[...], preferred_element_type=F32)
        turned = []
        for q in range(2):
            lanes = slice(q * share, (q + 1) * share)
            a, b = real[:, lanes], imag[:, lanes]
            ct, st = ct_ref[q, rows, :], st_ref[q, rows, :]
            turned.append((a * ct + b * st, a * st - b * ct))
        for p in range(blocks):
            total = acc[p, rows, :]
            for q in range(2):
                total = total + cos_ref[2 * step + q, p] * turned[q][0]
                total = total - sin_ref[2 * step + q, p] * turned[q][1]
            acc[p, rows, :] = total

    @pl.when(step == pl.num_programs(0) - 1)
    def _():
        scale = 1.0 / (2 * blocks * row_count)
        out_ref[...] = (acc[...] * scale).astype(BF16)


def call_long_filter(cos_block, sin_block, columns, cos_twist, sin_twist, first, second, table):
    blocks, row_count, share = columns.shape
    whole = lambda *shape: pl.BlockSpec(shape, lambda k: (0,) * len(shape))
    twist = pl.BlockSpec((2, row_count, share), lambda k: (k, 0, 0))
    piece = pl.BlockSpec((1, 2, row_count, share), lambda k: (k, 0, 0, 0))
    flops = 2 * blocks * 2 * (2 * row_count) ** 2 * (2 * share)
    return pl.pallas_call(
        long_filter,
        grid=(blocks,),
        out_shape=jax.ShapeDtypeStruct(columns.shape, BF16),
        in_specs=[
            pl.BlockSpec(memory_space=pltpu.SMEM),
            pl.BlockSpec(memory_space=pltpu.SMEM),
            whole(blocks, row_count, share),
            twist,
            twist,
            piece,
            piece,
            whole(2 * row_count, 2 * row_count),
        ],
        out_specs=whole(blocks, row_count, share),
        scratch_shapes=[
            pltpu.VMEM((blocks, row_count, share), F32),
            pltpu.VMEM((2 * row_count, 2 * share), BF16),
            pltpu.VMEM((2 * row_count, 2 * share), BF16),
        ],
        compiler_params=pltpu.CompilerParams(vmem_limit_bytes=56 * 2**20),
        cost_estimate=pl.CostEstimate(flops=flops, bytes_accessed=40 * 2**20, transcendentals=0),
    )(cos_block, sin_block, columns, cos_twist, sin_twist, first, second, table)


def on_device(tokens, w_in, w_short, skip_gain, filter_spectra, w_out):
    row_count = tokens.shape[0]
    channels = w_in.shape[2]
    seq_count = lax.axis_size("seq")
    bin_count = 2 * seq_count
    share = channels // seq_count
    fft_length = bin_count * row_count

    first_filter = spread_filter(filter_spectra, 0)
    gathered = lax.all_gather(tokens, "ch", axis=1, tiled=True)
    gathered, first_filter = lax.optimization_barrier((gathered, first_filter))
    second_filter = spread_filter(filter_spectra, 1)
    projected = [
        jnp.dot(gathered, w_in[:, s], preferred_element_type=F32).astype(BF16) for s in range(3)
    ]
    before = shifted(jnp.stack([p[row_count - 2 :] for p in projected]), "seq", 1)

    def stream(s):
        extended = jnp.concatenate([before[s], projected[s]], 0).astype(F32)
        taps = w_short[:, s]
        return taps[0] * extended[2:] + taps[1] * extended[1:-1] + taps[2] * extended[:-2]

    signal = (stream(0) * stream(2)).astype(BF16)
    signal, second_filter = lax.optimization_barrier((signal, second_filter))
    second_gate = stream(1)

    columns = lax.all_to_all(
        signal.reshape(row_count, seq_count, share).transpose(1, 0, 2),
        "seq",
        split_axis=0,
        concat_axis=0,
        tiled=True,
    )
    classes = jnp.arange(bin_count, dtype=jnp.int32)
    cos_block, sin_block = phases(classes, jnp.arange(seq_count, dtype=jnp.int32), bin_count)
    cos_twist, sin_twist = phases(classes, jnp.arange(row_count, dtype=jnp.int32), fft_length)
    twist_shape = (bin_count, row_count, share)
    convolved = call_long_filter(
        cos_block,
        sin_block,
        columns,
        jnp.broadcast_to(cos_twist[:, :, None], twist_shape),
        jnp.broadcast_to(sin_twist[:, :, None], twist_shape),
        first_filter,
        second_filter,
        jnp.asarray(dense_transform(row_count)),
    )
    owners = lax.axis_size("ch")
    half = row_count // (2 * owners)

    def rows_of(array, h, axis):
        shape = array.shape[:axis] + (owners, 2, half) + array.shape[axis + 1 :]
        picked = lax.index_in_dim(array.reshape(shape), h, axis + 1, keepdims=False)
        return picked.reshape(array.shape[:axis] + (owners * half,) + array.shape[axis + 1 :])

    outs = []
    for h in range(2):
        back = lax.all_to_all(
            rows_of(convolved, h, 1), "seq", split_axis=0, concat_axis=0, tiled=True
        )
        back = back.transpose(1, 0, 2).reshape(owners * half, channels).astype(F32)
        response = back + skip_gain * rows_of(signal, h, 0).astype(F32)
        gated_out = (rows_of(second_gate, h, 0) * response).astype(BF16)
        outs.append(
            lax.psum_scatter(
                jnp.dot(gated_out, w_out, preferred_element_type=F32).astype(BF16),
                "ch",
                scatter_dimension=0,
                tiled=True,
            )
        )
    return jnp.concatenate(outs, 0)


def solution(mesh):
    return jax.shard_map(
        on_device,
        mesh=mesh,
        in_specs=(
            P("seq", "ch"),
            P(None, None, "ch"),
            P(None, None, "ch"),
            P("ch"),
            P(None, "seq", None, "ch"),
            P("ch", None),
        ),
        out_specs=P(("seq", "ch"), None),
        check_vma=False,
    )
```

```python
import math

import jax
import jax.numpy as jnp
import ml_dtypes
import numpy as np
from jax import lax
from jax.experimental import pallas as pl
from jax.experimental.pallas import tpu as pltpu
from jax.sharding import PartitionSpec as P

TWO_PI = 2.0 * math.pi
BF16 = jnp.bfloat16
F32 = jnp.float32


def shifted(array, axis, by):
    count = lax.axis_size(axis)
    pairs = [(i, i + by) for i in range(count) if 0 <= i + by < count]
    return lax.ppermute(array, axis, pairs)


def dense_transform(size):
    product = np.outer(np.arange(size), np.arange(size)) % size
    angle = product * (TWO_PI / size)
    cos, sin = np.cos(angle), np.sin(angle)
    return np.block([[cos, sin], [-sin, cos]]).astype(ml_dtypes.bfloat16)


def phases(left, right, modulus):
    product = left[:, None] * right[None, :] % modulus
    angle = product.astype(F32) * (TWO_PI / modulus)
    return jnp.cos(angle), jnp.sin(angle)


def to_share(filter_part):
    parts, row_count, channels = filter_part.shape
    seq_count = lax.axis_size("seq")
    pieces = filter_part.reshape(parts, row_count, seq_count, channels // seq_count)
    return pieces.transpose(2, 0, 1, 3)


def exchanged(pieces):
    return lax.all_to_all(pieces, "seq", split_axis=0, concat_axis=0, tiled=True)


def long_filter(cos_ref, sin_ref, x_ref, ct_ref, st_ref, hr_ref, hi_ref, table_ref, out_ref, acc, left, right):
    blocks, row_count, share = x_ref.shape
    step = pl.program_id(0)
    chunk, tile = 64, 512

    @pl.when(step == 0)
    def _():
        acc[...] = jnp.zeros_like(acc)

    @pl.loop(0, row_count // chunk)
    def _(c):
        rows = pl.ds(pl.multiple_of(c * chunk, chunk), chunk)
        below = pl.ds(pl.multiple_of(row_count + c * chunk, chunk), chunk)
        x = [x_ref[p, rows, :].astype(F32) for p in range(blocks)]
        for q in range(2):
            real = x[0]
            imag = jnp.zeros_like(real)
            for p in range(1, blocks):
                real = real + cos_ref[2 * step + q, p] * x[p]
                imag = imag - sin_ref[2 * step + q, p] * x[p]
            ct, st = ct_ref[q, rows, :], st_ref[q, rows, :]
            lanes = slice(q * share, (q + 1) * share)
            left[rows, lanes] = (real * ct + imag * st).astype(BF16)
            left[below, lanes] = (imag * ct - real * st).astype(BF16)

    @pl.loop(0, row_count // tile)
    def _(m):
        rows = pl.ds(pl.multiple_of(m * tile, tile), tile)
        below = pl.ds(pl.multiple_of(row_count + m * tile, tile), tile)
        real = jnp.dot(table_ref[rows, :], left[...], preferred_element_type=F32)
        imag = jnp.dot(table_ref[below, :], left[...], preferred_element_type=F32)
        for q in range(2):
            lanes = slice(q * share, (q + 1) * share)
            a, b = real[:, lanes], imag[:, lanes]
            hr, hi = hr_ref[q, 0, rows, :].astype(F32), hi_ref[q, 0, rows, :].astype(F32)
            right[rows, lanes] = (a * hr - b * hi).astype(BF16)
            right[below, lanes] = (-(a * hi + b * hr)).astype(BF16)

    @pl.loop(0, row_count // tile)
    def _(m):
        rows = pl.ds(pl.multiple_of(m * tile, tile), tile)
        below = pl.ds(pl.multiple_of(row_count + m * tile, tile), tile)
        real = jnp.dot(table_ref[rows, :], right[...], preferred_element_type=F32)
        imag = jnp.dot(table_ref[below, :], right[...], preferred_element_type=F32)
        turned = []
        for q in range(2):
            lanes = slice(q * share, (q + 1) * share)
            a, b = real[:, lanes], imag[:, lanes]
            ct, st = ct_ref[q, rows, :], st_ref[q, rows, :]
            turned.append((a * ct + b * st, a * st - b * ct))
        for p in range(blocks):
            total = acc[p, rows, :]
            for q in range(2):
                total = total + cos_ref[2 * step + q, p] * turned[q][0]
                total = total - sin_ref[2 * step + q, p] * turned[q][1]
            acc[p, rows, :] = total

    @pl.when(step == pl.num_programs(0) - 1)
    def _():
        scale = 1.0 / (2 * blocks * row_count)
        out_ref[...] = (acc[...] * scale).astype(BF16)


def call_long_filter(cos_block, sin_block, columns, cos_twist, sin_twist, hr, hi, table):
    blocks, row_count, share = columns.shape
    whole = lambda *shape: pl.BlockSpec(shape, lambda k: (0,) * len(shape))
    twist = pl.BlockSpec((2, row_count, share), lambda k: (k, 0, 0))
    last = hi.shape[1] - 1
    flops = blocks * 2 * (2 * row_count) ** 2 * (2 * share)
    return pl.pallas_call(
        long_filter,
        grid=(blocks // 2,),
        out_shape=jax.ShapeDtypeStruct(columns.shape, BF16),
        in_specs=[
            pl.BlockSpec(memory_space=pltpu.SMEM),
            pl.BlockSpec(memory_space=pltpu.SMEM),
            whole(blocks, row_count, share),
            twist,
            twist,
            pl.BlockSpec((2, 1, row_count, share), lambda k: (k, 0, 0, 0)),
            pl.BlockSpec((2, 1, row_count, share), lambda k: (k, last, 0, 0)),
            whole(2 * row_count, 2 * row_count),
        ],
        out_specs=whole(blocks, row_count, share),
        scratch_shapes=[
            pltpu.VMEM((blocks, row_count, share), F32),
            pltpu.VMEM((2 * row_count, 2 * share), BF16),
            pltpu.VMEM((2 * row_count, 2 * share), BF16),
        ],
        compiler_params=pltpu.CompilerParams(vmem_limit_bytes=56 * 2**20),
        cost_estimate=pl.CostEstimate(flops=flops, bytes_accessed=24 * 2**20, transcendentals=0),
    )(cos_block, sin_block, columns, cos_twist, sin_twist, hr, hi, table)


def on_device(tokens, w_in, w_short, skip_gain, filter_spectra, w_out):
    row_count = tokens.shape[0]
    channels = w_in.shape[2]
    seq_count = lax.axis_size("seq")
    bin_count = 2 * seq_count
    share = channels // seq_count
    fft_length = bin_count * row_count

    first_filter = exchanged(to_share(filter_spectra[:, 0]))
    classes = jnp.arange(bin_count, dtype=jnp.int32)
    cos_block, sin_block = phases(classes, jnp.arange(seq_count, dtype=jnp.int32), bin_count)
    cos_twist, sin_twist = phases(classes, jnp.arange(row_count, dtype=jnp.int32), fft_length)
    cos_twist, sin_twist = cos_twist[:, :, None], sin_twist[:, :, None]
    twist_shape = (seq_count, row_count, share)
    twists = [
        jnp.broadcast_to(table[parity::2], twist_shape)
        for parity in range(2)
        for table in (cos_twist, sin_twist)
    ]

    gathered = lax.all_gather(tokens, "ch", axis=1, tiled=True)
    late = to_share(filter_spectra[1:, 1])
    gathered, first_filter, twists, late = lax.optimization_barrier(
        (gathered, first_filter, twists, late)
    )
    second_real = exchanged(to_share(filter_spectra[:1, 1]))
    projected = [
        jnp.dot(gathered, w_in[:, s], preferred_element_type=F32).astype(BF16) for s in range(3)
    ]
    before = shifted(jnp.stack([p[row_count - 2 :] for p in projected]), "seq", 1)

    def stream(s):
        extended = jnp.concatenate([before[s], projected[s]], 0).astype(F32)
        taps = w_short[:, s]
        return taps[0] * extended[2:] + taps[1] * extended[1:-1] + taps[2] * extended[:-2]

    signal = (stream(0) * stream(2)).astype(BF16)
    signal, second_real = lax.optimization_barrier((signal, second_real))
    second_gate = stream(1)

    columns = lax.all_to_all(
        signal.reshape(row_count, seq_count, share).transpose(1, 0, 2),
        "seq",
        split_axis=0,
        concat_axis=0,
        tiled=True,
    )
    columns, late = lax.optimization_barrier((columns, late))
    second_imag = exchanged(late)
    table = jnp.asarray(dense_transform(row_count))
    filters = ((first_filter, first_filter), (second_real, second_imag))
    shares = [
        call_long_filter(
            cos_block[parity::2],
            sin_block[parity::2],
            columns,
            twists[2 * parity],
            twists[2 * parity + 1],
            *filters[parity],
            table,
        )
        for parity in range(2)
    ]
    convolved = (shares[0].astype(F32) + shares[1].astype(F32)).astype(BF16)

    owners = lax.axis_size("ch")
    half = row_count // (2 * owners)

    def rows_of(array, h, axis):
        shape = array.shape[:axis] + (owners, 2, half) + array.shape[axis + 1 :]
        picked = lax.index_in_dim(array.reshape(shape), h, axis + 1, keepdims=False)
        return picked.reshape(array.shape[:axis] + (owners * half,) + array.shape[axis + 1 :])

    outs = []
    backs = [exchanged(rows_of(convolved, h, 1)) for h in range(2)]
    for h in range(2):
        back = backs[h]
        if h:
            back, product = lax.optimization_barrier((back, product[:16, :128]))
        back = back.transpose(1, 0, 2).reshape(owners * half, channels).astype(F32)
        response = back + skip_gain * rows_of(signal, h, 0).astype(F32)
        gated_out = (rows_of(second_gate, h, 0) * response).astype(BF16)
        product = jnp.dot(gated_out, w_out, preferred_element_type=F32).astype(BF16)
        outs.append(lax.psum_scatter(product, "ch", scatter_dimension=0, tiled=True))
    return jnp.concatenate(outs, 0)


def solution(mesh):
    return jax.shard_map(
        on_device,
        mesh=mesh,
        in_specs=(
            P("seq", "ch"),
            P(None, None, "ch"),
            P(None, None, "ch"),
            P("ch"),
            P(None, "seq", None, "ch"),
            P("ch", None),
        ),
        out_specs=P(("seq", "ch"), None),
        check_vma=False,
    )
```
